32 devices in a mesh: lat: 4 (over y, x), lon: 8 (over z, core).
Axes of the slice: x: 2, y: 2, z: 4, core: 2. Of those that a mesh axis runs over, the one named last changes fastest.
Arguments:
- tokens: bfloat16 [48, 384, 512], P('lat', 'lon'), may hold values from -6 to 6
- fine_qkv: bfloat16 [512, 1536], replicated, may hold values from -12 to 12
- fine_out: bfloat16 [512, 512], replicated, may hold values from -0.25 to 0.25
- fine_up: bfloat16 [512, 2048], replicated, may hold values from -0.25 to 0.25
- fine_down: bfloat16 [2048, 512], replicated, may hold values from -0.125 to 0.125
- merge_weight: bfloat16 [2048, 1024], replicated, may hold values from -0.125 to 0.125
- coarse_qkv: bfloat16 [1024, 3072], P(None, 'lon'), may hold values from -12 to 12
- coarse_out: bfloat16 [1024, 1024], P(None, 'lon'), may hold values from -0.1875 to 0.1875
- coarse_up: bfloat16 [1024, 4096], P(None, 'lon'), may hold values from -0.1875 to 0.1875
- coarse_down: bfloat16 [1024, 4096], P(None, 'lon'), may hold values from -0.09375 to 0.09375
- split_weight: bfloat16 [1024, 2048], replicated, may hold values from -0.1875 to 0.1875
Outputs:
- fine_result: bfloat16 [48, 384, 512], P('lat', 'lon')
The draws below stay inside these ranges and needn't reach their ends.
All inputs are finite; a program needn't handle non-finite values.
Results may differ from the reference program's by a relative error of at most 0.014.
Values may be sent and summed in bfloat16 or wider, within the bound.
A program may use at most 128 MiB of HBM per device.

```python
import jax
import jax.numpy as jnp
from jax import lax

D0 = 512
D1 = 1024
HID0 = 2048
HID1 = 4096
HD = 64
WH = 6
WW = 12
HEADS0 = 8
HEADS1 = 16
SH = 3
SW = 6
NH = 48
NW = 384


def head_columns(base_key, width, head_count):
    columns = jax.random.normal(base_key, (width, head_count, 3, HD), jnp.float32)
    return jnp.clip(columns, -6.0, 6.0) * width ** (-0.5)


def draw_fine_qkv(key, part):
    key = jax.random.fold_in(key, 11)
    base_key = jax.random.fold_in(key, 0)
    columns = head_columns(base_key, D0, HEADS0)
    return columns.reshape(D0, 3 * D0).astype(jnp.bfloat16)


def draw_coarse_qkv(key, part):
    key = jax.random.fold_in(key, 12)
    base_key = jax.random.fold_in(key, 0)
    columns = head_columns(base_key, D1, HEADS1)
    return columns.reshape(D1, 3 * D1).astype(jnp.bfloat16)


def block_levels(own_key, dims, pieces, least, largest):
    def one(axis_at, shards_of):
        heights = jax.random.uniform(jax.random.fold_in(jax.random.fold_in(own_key, 6), axis_at), (shards_of,), jnp.float32, least / len(pieces), largest / len(pieces))
        return jnp.repeat(jnp.exp(heights), dims[axis_at] // shards_of).reshape((-1,) + (1,) * (len(dims) - axis_at - 1))

    factor_of = one(*pieces[0])
    for cut in pieces[1:]:
        factor_of = factor_of * one(*cut)
    return factor_of


def noise(own_key, dims, deviation, bound, cuts=(), kind=jnp.bfloat16):
    drawn = deviation * jax.random.normal(own_key, dims, jnp.float32)
    if cuts:
        drawn = drawn * block_levels(own_key, dims, cuts, -0.22, 0.18)
    return jnp.clip(drawn, -bound, bound).astype(kind)


def setup_inputs(seed: int = 0) -> dict:
    seeds = jax.random.split(jax.random.key(seed), 12)
    return {
        "tokens": noise(seeds[0], (NH, NW, D0), 1.0, 6.0, ((0, 4), (1, 8))),
        "fine_qkv": draw_fine_qkv(jax.random.fold_in(seeds[11], 71), 0),
        "fine_out": noise(seeds[2], (D0, D0), D0 ** -0.5, 0.25),
        "fine_up": noise(seeds[3], (D0, HID0), D0 ** -0.5, 0.25),
        "fine_down": noise(seeds[4], (HID0, D0), HID0 ** -0.5, 0.125),
        "merge_weight": noise(seeds[5], (4 * D0, D1), (4 * D0) ** -0.5, 0.125),
        "coarse_qkv": draw_coarse_qkv(jax.random.fold_in(seeds[11], 71), 0),
        "coarse_out": noise(seeds[7], (D1, D1), D1 ** -0.5, 0.1875, ((1, 8),)),
        "coarse_up": noise(seeds[8], (D1, HID1), D1 ** -0.5, 0.1875, ((1, 8),)),
        "coarse_down": noise(seeds[9], (D1, HID1), HID1 ** -0.5, 0.09375, ((1, 8),)),
        "split_weight": noise(seeds[10], (D1, 4 * D0), D1 ** -0.5, 0.1875),
    }


def layer_norm(values):
    average = lax.optimization_barrier(jnp.mean(values, axis=-1, keepdims=True))
    centred = values - average
    spread = lax.optimization_barrier(jnp.mean(centred * centred, axis=-1, keepdims=True))
    return centred * lax.rsqrt(spread + 1e-05)

def project(operand, matrix):
    flattened = operand.reshape(-1, operand.shape[-1])
    result = jnp.dot(flattened, matrix, preferred_element_type=jnp.float32)
    return result.reshape(operand.shape[:-1] + (matrix.shape[1],))

def project_back(operand, matrix):
    flattened = operand.reshape(-1, operand.shape[-1])
    result = jnp.dot(flattened, matrix.T, preferred_element_type=jnp.float32)
    return result.reshape(operand.shape[:-1] + (matrix.shape[0],))

def window_attend(packed, labels, head_count):
    row_count, col_count = (packed.shape[0], packed.shape[1])
    row_wins, col_wins = (row_count // WH, col_count // WW)
    grouped = packed.astype(jnp.float32).reshape(row_wins, WH, col_wins, WW, head_count, 3, HD)
    grouped = grouped.transpose(0, 2, 4, 5, 1, 3, 6).reshape(row_wins, col_wins, head_count, 3, WH * WW, HD)
    queries = grouped[:, :, :, 0]
    key_rows = grouped[:, :, :, 1]
    value_rows = grouped[:, :, :, 2]
    scores = jnp.einsum('abhqd,abhkd->abhqk', queries, key_rows, precision=lax.Precision.HIGHEST) * HD ** (-0.5)
    if labels is not None:
        token_labels = jnp.broadcast_to(labels.reshape(row_wins, WH, 1), (row_wins, WH, WW)).reshape(row_wins, 1, 1, WH * WW)
        same_region = token_labels[..., :, None] == token_labels[..., None, :]
        scores = jnp.where(same_region, scores, -jnp.inf)
    row_max = lax.optimization_barrier(jnp.max(scores, axis=-1, keepdims=True))
    weights = jnp.exp(scores - row_max)
    normed_probs = (weights / lax.optimization_barrier(jnp.sum(weights, axis=-1, keepdims=True))).astype(jnp.bfloat16)
    mixture = jnp.einsum('abhqk,abhkd->abhqd', normed_probs.astype(jnp.float32), value_rows, precision=lax.Precision.HIGHEST).astype(jnp.bfloat16)
    mixture = mixture.reshape(row_wins, col_wins, head_count, WH, WW, HD).transpose(0, 3, 1, 4, 2, 5)
    return mixture.reshape(row_count, col_count, head_count * HD)

def reference(tokens, fine_qkv, fine_out, fine_up, fine_down, merge_weight, coarse_qkv, coarse_out, coarse_up, coarse_down, split_weight):
    stream = tokens.astype(jnp.float32)
    normed = layer_norm(stream).astype(jnp.bfloat16)
    rolled = jnp.roll(normed, (-SH, -SW), axis=(0, 1))
    packed = project(rolled, fine_qkv).astype(jnp.bfloat16)
    anchor = (jnp.arange(NH, dtype=jnp.int32) + SH) % NH
    labels = (anchor < SH).astype(jnp.int32)
    attended = jnp.roll(window_attend(packed, labels, HEADS0), (SH, SW), axis=(0, 1))
    stream = stream + project(attended, fine_out)
    hidden = jax.nn.gelu(project(layer_norm(stream).astype(jnp.bfloat16), fine_up), approximate=False).astype(jnp.bfloat16)
    skip_tokens = (stream + project(hidden, fine_down)).astype(jnp.bfloat16)
    merged = skip_tokens.reshape(NH // 2, 2, NW // 2, 2, D0).transpose(0, 2, 1, 3, 4).reshape(NH // 2, NW // 2, 4 * D0)
    coarse = project(layer_norm(merged.astype(jnp.float32)).astype(jnp.bfloat16), merge_weight).astype(jnp.bfloat16)
    level_state = coarse.astype(jnp.float32)
    packed = project(layer_norm(level_state).astype(jnp.bfloat16), coarse_qkv).astype(jnp.bfloat16)
    level_state = level_state + project_back(window_attend(packed, None, HEADS1), coarse_out)
    hidden = jax.nn.gelu(project(layer_norm(level_state).astype(jnp.bfloat16), coarse_up), approximate=False).astype(jnp.bfloat16)
    level_out = (level_state + project_back(hidden, coarse_down)).astype(jnp.bfloat16)
    expanded = project(level_out, split_weight).reshape(NH // 2, NW // 2, 2, 2, D0).transpose(0, 2, 1, 3, 4).reshape(NH, NW, D0)
    return (skip_tokens.astype(jnp.float32) + layer_norm(expanded)).astype(jnp.bfloat16)
```

```python
import functools

import jax
import jax.numpy as jnp
from jax import lax
from jax.experimental import pallas as pl
from jax.experimental.pallas import tpu as pltpu
from jax.sharding import PartitionSpec as P

HD = 64
WH = 6
WW = 12
SH = 3
SW = 6


def shifted_2(block, axis, distance):
    devices = range(lax.axis_size(axis))
    route = [((i - distance) % len(devices), i) for i in devices]
    return lax.ppermute(block, axis, route)


def layer_norm(values):
    average = jnp.mean(values, axis=-1, keepdims=True)
    centred = values - average
    spread = jnp.mean(centred * centred, axis=-1, keepdims=True)
    return centred * lax.rsqrt(spread + 1e-05)


def project(operand, matrix):
    flattened = operand.reshape(-1, operand.shape[-1])
    result = jnp.dot(flattened, matrix, preferred_element_type=jnp.float32)
    return result.reshape(operand.shape[:-1] + (matrix.shape[1],))


def project_back(operand, matrix):
    flattened = operand.reshape(-1, operand.shape[-1])
    result = lax.dot_general(
        flattened, matrix, (((1,), (1,)), ((), ())), preferred_element_type=jnp.float32
    )
    return result.reshape(operand.shape[:-1] + (matrix.shape[0],))


def window_attend(packed, labels, head_count):
    row_count, col_count = (packed.shape[0], packed.shape[1])
    row_wins, col_wins = (row_count // WH, col_count // WW)
    grouped = packed.reshape(row_wins, WH, col_wins, WW, head_count, 3, HD)
    grouped = grouped.transpose(0, 2, 4, 5, 1, 3, 6).reshape(
        row_wins, col_wins, head_count, 3, WH * WW, HD
    )
    queries = grouped[:, :, :, 0]
    key_rows = grouped[:, :, :, 1]
    value_rows = grouped[:, :, :, 2]
    scores = jnp.einsum(
        "abhqd,abhkd->abhqk", queries, key_rows, preferred_element_type=jnp.float32
    ) * HD ** (-0.5)
    if labels is not None:
        token_labels = jnp.broadcast_to(
            labels.reshape(row_wins, WH, 1), (row_wins, WH, WW)
        ).reshape(row_wins, 1, 1, WH * WW)
        same_region = token_labels[..., :, None] == token_labels[..., None, :]
        scores = jnp.where(same_region, scores, -jnp.inf)
    row_max = jnp.max(scores, axis=-1, keepdims=True)
    weights = jnp.exp(scores - row_max)
    normed_probs = (weights / jnp.sum(weights, axis=-1, keepdims=True)).astype(jnp.bfloat16)
    mixture = jnp.einsum(
        "abhqk,abhkd->abhqd", normed_probs, value_rows, preferred_element_type=jnp.float32
    ).astype(jnp.bfloat16)
    mixture = mixture.reshape(row_wins, col_wins, head_count, WH, WW, HD).transpose(
        0, 3, 1, 4, 2, 5
    )
    return mixture.reshape(row_count, col_count, head_count * HD)


def head_terms(normed, qkv_cols, out_cols):
    head_count = qkv_cols.shape[1] // (3 * HD)
    packed = project(normed, qkv_cols).astype(jnp.bfloat16)
    return project_back(window_attend(packed, None, head_count), out_cols)


def unit_terms(normed, up_cols, down_cols):
    hidden = jax.nn.gelu(project(normed, up_cols), approximate=False).astype(jnp.bfloat16)
    return project_back(hidden, down_cols)


BLK = 128
NT = (((1,), (1,)), ((), ()))


def softmax_mix(q, k, v, bias):
    scores = lax.dot_general(q, k, NT, preferred_element_type=jnp.float32) * HD ** (-0.5)
    if bias is not None:
        scores = scores + bias
    weights = jnp.exp(scores - jnp.max(scores, axis=-1, keepdims=True))
    probs = weights / jnp.sum(weights, axis=-1, keepdims=True)
    return jnp.dot(probs.astype(jnp.bfloat16), v, preferred_element_type=jnp.float32)


def fine_kernel(heads, qkv_ref, bias_ref, out_ref):
    bias = bias_ref[0]
    for pair in range(heads // 2):
        block = qkv_ref[0, :, pair * 6 * HD : (pair + 1) * 6 * HD]
        parts = [block[:, i * HD : (i + 1) * HD] for i in range(6)]
        mixed = [softmax_mix(*parts[3 * i : 3 * i + 3], bias) for i in range(2)]
        out_ref[0, :, pair * 2 * HD : (pair + 1) * 2 * HD] = jnp.concatenate(
            mixed, axis=1
        ).astype(jnp.bfloat16)


def fine_attend(qkv, bias):
    wins, size, width = qkv.shape
    per_row = wins // bias.shape[0]
    return pl.pallas_call(
        functools.partial(fine_kernel, width // (3 * HD)),
        out_shape=jax.ShapeDtypeStruct((wins, size, width // 3), jnp.bfloat16),
        grid=(wins,),
        in_specs=[
            pl.BlockSpec((1, size, width), lambda w: (w, 0, 0)),
            pl.BlockSpec((1, size, size), lambda w: (w // per_row, 0, 0)),
        ],
        out_specs=pl.BlockSpec((1, size, width // 3), lambda w: (w, 0, 0)),
        compiler_params=pltpu.CompilerParams(vmem_limit_bytes=32 * 2**20),
        cost_estimate=pl.CostEstimate(
            flops=4 * wins * size * size * width // 3,
            bytes_accessed=wins * size * width * 3,
            transcendentals=wins * size * size * width // (3 * HD),
        ),
    )(qkv, bias)


def coarse_attend_kernel(sets, lats, x_ref, *refs):
    out_ref = refs[-1]
    x = x_ref[...]
    size = WH * WW
    total = None
    for s in range(sets):
        a, b = refs[2 * s], refs[2 * s + 1]
        deep = b.shape[1] // 2
        place = [j // 2 + (j % 2) * (lats // 2) for j in range(lats)]
        cols = [
            jnp.concatenate([a[j, :deep] for j in range(lats)], axis=0),
            jnp.concatenate([a[j, deep:] for j in range(lats)], axis=0),
            jnp.concatenate([b[p, :deep] for p in place], axis=0),
        ]
        out_rows = jnp.concatenate([b[p, deep:] for p in place], axis=0)
        qkv = jnp.dot(x, jnp.concatenate(cols, axis=1), preferred_element_type=jnp.float32)
        rows = []
        for w in range(x.shape[0] // size):
            block = qkv[w * size : (w + 1) * size].astype(jnp.bfloat16)
            parts = [block[:, i * HD : (i + 1) * HD] for i in range(6)]
            rows.append(
                jnp.concatenate(
                    [softmax_mix(*parts[3 * i : 3 * i + 3], None) for i in range(2)], axis=1
                )
            )
        mixed = jnp.concatenate(rows, axis=0).astype(jnp.bfloat16)
        term = lax.dot_general(mixed, out_rows, NT, preferred_element_type=jnp.float32)
        total = term if total is None else total + term
    out_ref[...] = total


def coarse_attend(x, sets, lats):
    count, width = x.shape
    deep = sets[0].shape[1] // 3
    specs, operands = [pl.BlockSpec((count, width), lambda i: (0, 0))], [x]
    for one in sets:
        operands += [one, one]
        specs += [
            pl.BlockSpec((lats, deep, BLK), lambda i: (0, 2, 0)),
            pl.BlockSpec((lats, deep, BLK), lambda i: (1, 2, 0)),
        ]
    return pl.pallas_call(
        functools.partial(coarse_attend_kernel, len(sets), lats),
        out_shape=jax.ShapeDtypeStruct((count, width), jnp.float32),
        grid=(1,),
        in_specs=specs,
        out_specs=pl.BlockSpec((count, width), lambda i: (0, 0)),
        compiler_params=pltpu.CompilerParams(vmem_limit_bytes=48 * 2**20),
        cost_estimate=pl.CostEstimate(
            flops=8 * count * width * width,
            bytes_accessed=8 * width * width,
            transcendentals=count * WH * WW * 16,
        ),
    )(*operands)


def coarse_mlp_kernel(sets, x_ref, *refs):
    out_ref = refs[-1]
    x = x_ref[...]

    @pl.when(pl.program_id(0) == 0)
    def _():
        out_ref[...] = jnp.zeros_like(out_ref)

    total = out_ref[...]
    for s in range(0, sets, 2):
        up = jnp.concatenate([refs[2 * s][0], refs[2 * s + 2][0]], axis=1)
        down = jnp.concatenate([refs[2 * s + 1][0], refs[2 * s + 3][0]], axis=1)
        wide = jnp.dot(x, up, preferred_element_type=jnp.float32)
        hidden = (0.5 * wide * (1.0 + lax.erf(wide * 0.5**0.5))).astype(jnp.bfloat16)
        total = total + lax.dot_general(hidden, down, NT, preferred_element_type=jnp.float32)
    out_ref[...] = total


def coarse_mlp(x, sets, lats):
    count, width = x.shape
    specs, operands = [pl.BlockSpec((count, width), lambda j: (0, 0))], [x]
    for one in sets:
        operands += [one, one]
        specs += [
            pl.BlockSpec((1, width, BLK), lambda j: (j, 0, 0)),
            pl.BlockSpec((1, width, BLK), lambda j: (lats + j // 2 + (j % 2) * (lats // 2), 0, 0)),
        ]
    return pl.pallas_call(
        functools.partial(coarse_mlp_kernel, len(sets)),
        out_shape=jax.ShapeDtypeStruct((count, width), jnp.float32),
        grid=(lats,),
        in_specs=specs,
        out_specs=pl.BlockSpec((count, width), lambda j: (0, 0)),
        compiler_params=pltpu.CompilerParams(vmem_limit_bytes=48 * 2**20),
        cost_estimate=pl.CostEstimate(
            flops=16 * count * width * width,
            bytes_accessed=16 * width * width,
            transcendentals=count * 4 * width,
        ),
    )(*operands)


def swapped(block, axis, bit):
    return lax.ppermute(block, axis, [(i, i ^ bit) for i in range(lax.axis_size(axis))])


def gathered_weights(qkv, out, up, down):
    lats, lons = lax.axis_size("lat"), lax.axis_size("lon")
    own = lax.axis_index("lat")
    deep = qkv.shape[0] // lats
    half_a, half_b = [], []
    for j in range(lats):
        at = own ^ j
        rows = [lax.dynamic_slice_in_dim(qkv, at * deep, deep, 0)[:, i * BLK : (i + 1) * BLK] for i in range(3)]
        rows.append(lax.dynamic_slice_in_dim(out, at * deep, deep, 0))
        half_a.append(jnp.concatenate([lax.dynamic_slice_in_dim(up, at * BLK, BLK, 1)] + rows[:2], axis=0))
        half_b.append(jnp.concatenate([lax.dynamic_slice_in_dim(down, at * BLK, BLK, 1)] + rows[2:], axis=0))
    place = [j // 2 + (j % 2) * (lats // 2) for j in range(lats)]
    order_b = [place.index(p) for p in range(lats)]
    mine = jnp.stack(half_a + [half_b[j] for j in order_b])
    sets = [mine, swapped(mine, "lon", 1)]
    moving = jnp.stack([half_a[0], half_b[0]])
    bits = [1 << i for i in range(lats.bit_length() - 1)]
    for _ in range(lons // 2 - 1):
        moving = lax.ppermute(moving, "lon", [(i, (i + 2) % lons) for i in range(lons)])
        a, b = moving[:1], moving[1:]
        for bit_a, bit_b in zip(bits, bits[1:] + bits[:1]):
            a = jnp.concatenate([a, swapped(a, "lat", bit_a)], axis=0)
            b = jnp.concatenate([b, swapped(b, "lat", bit_b)], axis=0)
        full = jnp.concatenate([a, b], axis=0)
        sets += [full, swapped(full, "lon", 1)]
    return sets


def by_part(values, lats):
    own = lax.axis_index("lat")
    deep = values.shape[1] // lats
    return jnp.concatenate(
        [lax.dynamic_slice_in_dim(values, (own ^ j) * deep, deep, 1) for j in range(lats)], axis=1
    )


def local_level(coarse, sets):
    lats = lax.axis_size("lat")
    row_wins, col_wins = (coarse.shape[0] // WH, coarse.shape[1] // WW)
    tokens = (
        coarse.reshape(row_wins, WH, col_wins, WW, -1)
        .transpose(0, 2, 1, 3, 4)
        .reshape(-1, coarse.shape[-1])
    )
    normed = by_part(layer_norm(tokens).astype(jnp.bfloat16), lats)
    tokens = tokens + by_part(coarse_attend(normed, sets, lats), lats)
    tokens = tokens + coarse_mlp(layer_norm(tokens).astype(jnp.bfloat16), sets, lats)
    return (
        tokens.astype(jnp.bfloat16)
        .reshape(row_wins, col_wins, WH, WW, -1)
        .transpose(0, 2, 1, 3, 4)
        .reshape(coarse.shape)
    )


def per_device(
    tokens,
    fine_qkv,
    fine_out,
    fine_up,
    fine_down,
    merge_weight,
    coarse_qkv,
    coarse_out,
    coarse_up,
    coarse_down,
    split_weight,
):
    band_rows, band_cols = (tokens.shape[0], tokens.shape[1])
    total_rows = band_rows * lax.axis_size("lat")
    lat_index = lax.axis_index("lat")
    whole_weights = (
        coarse_up.shape[1] == lax.axis_size("lat") * BLK and coarse_qkv.shape[1] == 3 * BLK
    )
    if whole_weights:
        sets = gathered_weights(coarse_qkv, coarse_out, coarse_up, coarse_down)
    stream = tokens.astype(jnp.float32)
    normed = layer_norm(stream).astype(jnp.bfloat16)
    below_rows = shifted_2(normed[:SH], "lat", -1)
    shifted = jnp.concatenate([normed[SH:], below_rows], axis=0)
    east_cols = shifted_2(shifted[:, :SW], "lon", -1)
    shifted = jnp.concatenate([shifted[:, SW:], east_cols], axis=1)
    anchor = (lat_index * band_rows + jnp.arange(band_rows, dtype=jnp.int32) + SH) % total_rows
    labels = (anchor < SH).astype(jnp.int32)
    row_wins, col_wins = (band_rows // WH, band_cols // WW)
    window_labels = jnp.repeat(labels.reshape(row_wins, WH), WW, axis=1)
    same_region = window_labels[:, :, None] == window_labels[:, None, :]
    bias = jnp.where(same_region, 0.0, -jnp.inf).astype(jnp.float32)
    shifted = (
        shifted.reshape(row_wins, WH, col_wins, WW, -1)
        .transpose(0, 2, 1, 3, 4)
        .reshape(row_wins * col_wins, WH * WW, -1)
    )
    attended = fine_attend(project(shifted, fine_qkv).astype(jnp.bfloat16), bias)
    attended = (
        attended.reshape(row_wins, col_wins, WH, WW, -1)
        .transpose(0, 2, 1, 3, 4)
        .reshape(band_rows, band_cols, -1)
    )
    above_rows = shifted_2(attended[band_rows - SH :], "lat", 1)
    attended = jnp.concatenate([above_rows, attended[: band_rows - SH]], axis=0)
    west_cols = shifted_2(attended[:, band_cols - SW :], "lon", 1)
    attended = jnp.concatenate([west_cols, attended[:, : band_cols - SW]], axis=1)
    stream = stream + project(attended, fine_out)
    hidden = jax.nn.gelu(
        project(layer_norm(stream).astype(jnp.bfloat16), fine_up), approximate=False
    ).astype(jnp.bfloat16)
    skip_tokens = (stream + project(hidden, fine_down)).astype(jnp.bfloat16)
    coarse_rows, coarse_cols = (band_rows // 2, band_cols // 2)
    merged = (
        skip_tokens.reshape(coarse_rows, 2, coarse_cols, 2, -1)
        .transpose(0, 2, 1, 3, 4)
        .reshape(coarse_rows, coarse_cols, -1)
    )
    coarse = project(
        layer_norm(merged.astype(jnp.float32)).astype(jnp.bfloat16), merge_weight
    ).astype(jnp.bfloat16)
    coarse_float = coarse.astype(jnp.float32)
    if whole_weights:
        level_state = local_level(coarse_float, sets)
    else:
        gathered = lax.all_gather(
            layer_norm(coarse_float).astype(jnp.bfloat16), "lon", axis=1, tiled=True
        )
        level_state = coarse_float + lax.psum_scatter(
            head_terms(gathered, coarse_qkv, coarse_out).astype(jnp.bfloat16),
            "lon",
            scatter_dimension=1,
            tiled=True,
        ).astype(jnp.float32)
        unit_total = unit_terms(
            lax.all_gather(layer_norm(level_state).astype(jnp.bfloat16), "lon", axis=1, tiled=True),
            coarse_up,
            coarse_down,
        )
        level_state = (
            level_state
            + lax.psum_scatter(
                unit_total.astype(jnp.bfloat16), "lon", scatter_dimension=1, tiled=True
            ).astype(jnp.float32)
        ).astype(jnp.bfloat16)
    expanded = project(level_state, split_weight)
    expanded = (
        expanded.reshape(coarse_rows, coarse_cols, 2, 2, -1)
        .transpose(0, 2, 1, 3, 4)
        .reshape(band_rows, band_cols, -1)
    )
    return (skip_tokens.astype(jnp.float32) + layer_norm(expanded)).astype(jnp.bfloat16)


def solution(mesh):
    return jax.shard_map(
        per_device,
        mesh=mesh,
        in_specs=(
            P("lat", "lon", None),
            P(),
            P(),
            P(),
            P(),
            P(),
            P(None, "lon"),
            P(None, "lon"),
            P(None, "lon"),
            P(None, "lon"),
            P(),
        ),
        out_specs=P("lat", "lon", None),
        check_vma=False,
    )
```

```python
import functools

import jax
import jax.numpy as jnp
from jax import lax
from jax.experimental import pallas as pl
from jax.experimental.pallas import tpu as pltpu
from jax.sharding import PartitionSpec as P

HD = 64
WH = 6
WW = 12
SH = 3
SW = 6


def shifted_2(block, axis, distance):
    devices = range(lax.axis_size(axis))
    route = [((i - distance) % len(devices), i) for i in devices]
    return lax.ppermute(block, axis, route)


def layer_norm(values):
    average = jnp.mean(values, axis=-1, keepdims=True)
    centred = values - average
    spread = jnp.mean(centred * centred, axis=-1, keepdims=True)
    return centred * lax.rsqrt(spread + 1e-05)


def project(operand, matrix):
    flattened = operand.reshape(-1, operand.shape[-1])
    result = jnp.dot(flattened, matrix, preferred_element_type=jnp.float32)
    return result.reshape(operand.shape[:-1] + (matrix.shape[1],))


def project_back(operand, matrix):
    flattened = operand.reshape(-1, operand.shape[-1])
    result = lax.dot_general(
        flattened, matrix, (((1,), (1,)), ((), ())), preferred_element_type=jnp.float32
    )
    return result.reshape(operand.shape[:-1] + (matrix.shape[0],))


def window_attend(packed, labels, head_count):
    row_count, col_count = (packed.shape[0], packed.shape[1])
    row_wins, col_wins = (row_count // WH, col_count // WW)
    grouped = packed.reshape(row_wins, WH, col_wins, WW, head_count, 3, HD)
    grouped = grouped.transpose(0, 2, 4, 5, 1, 3, 6).reshape(
        row_wins, col_wins, head_count, 3, WH * WW, HD
    )
    queries = grouped[:, :, :, 0]
    key_rows = grouped[:, :, :, 1]
    value_rows = grouped[:, :, :, 2]
    scores = jnp.einsum(
        "abhqd,abhkd->abhqk", queries, key_rows, preferred_element_type=jnp.float32
    ) * HD ** (-0.5)
    if labels is not None:
        token_labels = jnp.broadcast_to(
            labels.reshape(row_wins, WH, 1), (row_wins, WH, WW)
        ).reshape(row_wins, 1, 1, WH * WW)
        same_region = token_labels[..., :, None] == token_labels[..., None, :]
        scores = jnp.where(same_region, scores, -jnp.inf)
    row_max = jnp.max(scores, axis=-1, keepdims=True)
    weights = jnp.exp(scores - row_max)
    normed_probs = (weights / jnp.sum(weights, axis=-1, keepdims=True)).astype(jnp.bfloat16)
    mixture = jnp.einsum(
        "abhqk,abhkd->abhqd", normed_probs, value_rows, preferred_element_type=jnp.float32
    ).astype(jnp.bfloat16)
    mixture = mixture.reshape(row_wins, col_wins, head_count, WH, WW, HD).transpose(
        0, 3, 1, 4, 2, 5
    )
    return mixture.reshape(row_count, col_count, head_count * HD)


def head_terms(normed, qkv_cols, out_cols):
    head_count = qkv_cols.shape[1] // (3 * HD)
    packed = project(normed, qkv_cols).astype(jnp.bfloat16)
    return project_back(window_attend(packed, None, head_count), out_cols)


def unit_terms(normed, up_cols, down_cols):
    hidden = jax.nn.gelu(project(normed, up_cols), approximate=False).astype(jnp.bfloat16)
    return project_back(hidden, down_cols)


BLK = 128
NT = (((1,), (1,)), ((), ()))


def softmax_mix(q, k, v, bias):
    scores = lax.dot_general(q, k, NT, preferred_element_type=jnp.float32) * HD ** (-0.5)
    if bias is not None:
        scores = scores + bias
    weights = jnp.exp(scores - jnp.max(scores, axis=-1, keepdims=True))
    probs = weights / jnp.sum(weights, axis=-1, keepdims=True)
    return jnp.dot(probs.astype(jnp.bfloat16), v, preferred_element_type=jnp.float32)


def fine_kernel(heads, qkv_ref, bias_ref, out_ref):
    bias = bias_ref[0]
    for pair in range(heads // 2):
        block = qkv_ref[0, :, pair * 6 * HD : (pair + 1) * 6 * HD]
        parts = [block[:, i * HD : (i + 1) * HD] for i in range(6)]
        mixed = [softmax_mix(*parts[3 * i : 3 * i + 3], bias) for i in range(2)]
        out_ref[0, :, pair * 2 * HD : (pair + 1) * 2 * HD] = jnp.concatenate(
            mixed, axis=1
        ).astype(jnp.bfloat16)


def fine_attend(qkv, bias):
    wins, size, width = qkv.shape
    per_row = wins // bias.shape[0]
    return pl.pallas_call(
        functools.partial(fine_kernel, width // (3 * HD)),
        out_shape=jax.ShapeDtypeStruct((wins, size, width // 3), jnp.bfloat16),
        grid=(wins,),
        in_specs=[
            pl.BlockSpec((1, size, width), lambda w: (w, 0, 0)),
            pl.BlockSpec((1, size, size), lambda w: (w // per_row, 0, 0)),
        ],
        out_specs=pl.BlockSpec((1, size, width // 3), lambda w: (w, 0, 0)),
        compiler_params=pltpu.CompilerParams(vmem_limit_bytes=32 * 2**20),
        cost_estimate=pl.CostEstimate(
            flops=4 * wins * size * size * width // 3,
            bytes_accessed=wins * size * width * 3,
            transcendentals=wins * size * size * width // (3 * HD),
        ),
    )(qkv, bias)


def coarse_attend_kernel(x_ref, qkv_ref, rows_ref, a0_ref, a1_ref, b0_ref, b1_ref, own_ref, peer_ref, sum_ref):
    lat = lax.axis_index("lat")
    count, width = x_ref.shape
    size, deep = WH * WW, width // 4
    shifts = a0_ref.shape[0] // 2
    halves_a, halves_b = (a0_ref, a1_ref), (b0_ref, b1_ref)

    def mixed_heads(qkv):
        rows = []
        for w in range(count // size):
            block = qkv[w * size : (w + 1) * size].astype(jnp.bfloat16)
            parts = [block[:, i * HD : (i + 1) * HD] for i in range(6)]
            rows.append(
                jnp.concatenate(
                    [softmax_mix(*parts[3 * i : 3 * i + 3], None) for i in range(2)], axis=1
                )
            )
        return jnp.concatenate(rows, axis=0).astype(jnp.bfloat16)

    def columns(j):
        return pl.ds(pl.multiple_of((lat ^ j) * deep, deep), deep)

    mixed = mixed_heads(jnp.dot(x_ref[...], qkv_ref[...], preferred_element_type=jnp.float32))
    sum_ref[...] = lax.dot_general(mixed, rows_ref[...], NT, preferred_element_type=jnp.float32)
    for s in range(shifts):
        qkv = None
        for j in range(4):
            first = halves_a[j // 2][(j % 2) * shifts + s]
            second = halves_b[j % 2][(j // 2) * shifts + s]
            block = jnp.concatenate([first[:deep], first[deep:], second[:deep]], axis=1)
            term = jnp.dot(x_ref[:, columns(j)], block, preferred_element_type=jnp.float32)
            qkv = term if qkv is None else qkv + term
        mixed = mixed_heads(qkv)
        for j in range(4):
            out_rows = halves_b[j % 2][(j // 2) * shifts + s][deep:]
            sum_ref[:, columns(j)] += lax.dot_general(
                mixed, out_rows, NT, preferred_element_type=jnp.float32
            )
    own_ref[...] = sum_ref[: count // 2]
    peer_ref[...] = sum_ref[count // 2 :].astype(jnp.bfloat16)


def coarse_attend(x, qkv, out, moved):
    count, width = x.shape
    whole = pl.BlockSpec(memory_space=pltpu.VMEM)
    return pl.pallas_call(
        coarse_attend_kernel,
        out_shape=(
            jax.ShapeDtypeStruct((count // 2, width), jnp.float32),
            jax.ShapeDtypeStruct((count // 2, width), jnp.bfloat16),
        ),
        in_specs=[whole] * 7,
        out_specs=(whole, whole),
        scratch_shapes=[pltpu.VMEM((count, width), jnp.float32)],
        compiler_params=pltpu.CompilerParams(vmem_limit_bytes=40 * 2**20),
        cost_estimate=pl.CostEstimate(
            flops=4 * count * width * width,
            bytes_accessed=4 * width * width,
            transcendentals=count * WH * WW * 8,
        ),
    )(x, qkv, out, *moved)


def coarse_mlp_kernel(x_ref, base_ref, *refs):
    ups, downs, out_ref = refs[: len(refs) // 2], refs[len(refs) // 2 : -1], refs[-1]

    @pl.when(pl.program_id(0) == 0)
    def _():
        out_ref[...] = base_ref[...]

    def joined(parts):
        parts = [part[...].reshape(part.shape[-2:]) for part in parts]
        return parts[0] if len(parts) == 1 else jnp.concatenate(parts, axis=1)

    wide = jnp.dot(x_ref[...], joined(ups), preferred_element_type=jnp.float32)
    hidden = (0.5 * wide * (1.0 + lax.erf(wide * 0.5**0.5))).astype(jnp.bfloat16)
    out_ref[...] += lax.dot_general(hidden, joined(downs), NT, preferred_element_type=jnp.float32)


def coarse_mlp(x, base, steps, operands, specs):
    count, width = x.shape
    whole = pl.BlockSpec((count, width), lambda s: (0, 0))
    hidden = steps * 4 * BLK
    return pl.pallas_call(
        coarse_mlp_kernel,
        out_shape=jax.ShapeDtypeStruct((count, width), jnp.float32),
        grid=(steps,),
        in_specs=[whole, whole] + specs,
        out_specs=whole,
        compiler_params=pltpu.CompilerParams(vmem_limit_bytes=40 * 2**20),
        cost_estimate=pl.CostEstimate(
            flops=4 * count * width * hidden,
            bytes_accessed=4 * width * hidden,
            transcendentals=count * hidden,
        ),
    )(x, base, *operands)


def own_mlp(x, up, down):
    base = jnp.zeros(x.shape, jnp.float32)
    return coarse_mlp(x, base, 1, [up, down], [pl.BlockSpec(up.shape, lambda s: (0, 0))] * 2)


def moved_mlp(x, base, moved):
    a0, a1, b0, b1 = moved
    shifts = a0.shape[0] // 2
    low = pl.BlockSpec((1,) + a0.shape[1:], lambda s: (s, 0, 0))
    high = pl.BlockSpec((1,) + a0.shape[1:], lambda s: (shifts + s, 0, 0))
    operands = [a0, a0, a1, a1, b0, b1, b0, b1]
    return coarse_mlp(x, base, shifts, operands, [low, high, low, high, low, low, high, high])


def swapped(block, axis, bit):
    return lax.ppermute(block, axis, [(i, i ^ bit) for i in range(lax.axis_size(axis))])


def along_lon(a, b):
    lons = lax.axis_size("lon")
    both = jnp.stack([a, b])
    return [
        lax.ppermute(both, "lon", [(i, (i + shift) % lons) for i in range(lons)])
        for shift in range(2, lons, 2)
    ]


def first_swap(got):
    a = jnp.stack([one[0] for one in got])
    b = jnp.stack([one[1] for one in got])
    return (a, swapped(a, "lat", 1), b, swapped(b, "lat", 2))


def second_swap(a, ax, b, by):
    a0, b0 = jnp.concatenate([a, ax], axis=0), jnp.concatenate([b, by], axis=0)
    return (a0, swapped(a0, "lat", 2), b0, swapped(b0, "lat", 1))


def level_parts(qkv, out, up, down):
    lat = lax.axis_index("lat")
    deep = qkv.shape[0] // 4
    qkv = lax.dynamic_slice_in_dim(qkv, lat * deep, deep, 0)
    out = lax.dynamic_slice_in_dim(out, lat * deep, deep, 0)
    first = jnp.concatenate([qkv[:, :BLK], qkv[:, BLK : 2 * BLK]], axis=0)
    second = jnp.concatenate([qkv[:, 2 * BLK :], out], axis=0)
    up = lax.dynamic_slice_in_dim(up, lat * BLK, BLK, 1)
    return (first, second), (up, lax.dynamic_slice_in_dim(down, lat * BLK, BLK, 1))


def local_level(tokens, attend_moved, mlp_moved, qkv, out, up, down):
    count = tokens.shape[0]

    def shared(values):
        normed = layer_norm(values).astype(jnp.bfloat16)
        return jnp.concatenate([normed, swapped(normed, "lon", 1)], axis=0)

    own, peer = coarse_attend(shared(tokens), qkv, out, attend_moved)
    tokens = tokens + own + swapped(peer, "lon", 1).astype(jnp.float32)
    both = shared(tokens)
    total = own_mlp(both, up, down)
    for moved in mlp_moved:
        total = moved_mlp(both, total, moved)
    peer = swapped(total[count:].astype(jnp.bfloat16), "lon", 1)
    return (tokens + total[:count] + peer.astype(jnp.float32)).astype(jnp.bfloat16)


def per_device(
    tokens,
    fine_qkv,
    fine_out,
    fine_up,
    fine_down,
    merge_weight,
    coarse_qkv,
    coarse_out,
    coarse_up,
    coarse_down,
    split_weight,
):
    band_rows, band_cols = (tokens.shape[0], tokens.shape[1])
    total_rows = band_rows * lax.axis_size("lat")
    lat_index = lax.axis_index("lat")
    whole_weights = (
        lax.axis_size("lat") == 4 and coarse_up.shape[1] == 4 * BLK and coarse_qkv.shape[1] == 3 * BLK
    )
    if whole_weights:
        attend_part, mlp_part = level_parts(coarse_qkv, coarse_out, coarse_up, coarse_down)
        attend_moved, mlp_moved = (along_lon(*attend_part), along_lon(*mlp_part))
    stream = tokens.astype(jnp.float32)
    normed = layer_norm(stream).astype(jnp.bfloat16)
    below_rows = shifted_2(normed[:SH], "lat", -1)
    shifted = jnp.concatenate([normed[SH:], below_rows], axis=0)
    east_cols = shifted_2(shifted[:, :SW], "lon", -1)
    shifted = jnp.concatenate([shifted[:, SW:], east_cols], axis=1)
    anchor = (lat_index * band_rows + jnp.arange(band_rows, dtype=jnp.int32) + SH) % total_rows
    labels = (anchor < SH).astype(jnp.int32)
    row_wins, col_wins = (band_rows // WH, band_cols // WW)
    window_labels = jnp.repeat(labels.reshape(row_wins, WH), WW, axis=1)
    same_region = window_labels[:, :, None] == window_labels[:, None, :]
    bias = jnp.where(same_region, 0.0, -jnp.inf).astype(jnp.float32)
    shifted = (
        shifted.reshape(row_wins, WH, col_wins, WW, -1)
        .transpose(0, 2, 1, 3, 4)
        .reshape(row_wins * col_wins, WH * WW, -1)
    )
    packed = project(shifted, fine_qkv).astype(jnp.bfloat16)
    if whole_weights:
        packed, attend_moved = lax.optimization_barrier((packed, attend_moved))
        attend_moved = first_swap(attend_moved)
    attended = fine_attend(packed, bias)
    if whole_weights:
        near, middle, far = mlp_moved
        attended, attend_moved, near = lax.optimization_barrier((attended, attend_moved, near))
        attend_moved = second_swap(*attend_moved)
        near = first_swap([near])
    attended = (
        attended.reshape(row_wins, col_wins, WH, WW, -1)
        .transpose(0, 2, 1, 3, 4)
        .reshape(band_rows, band_cols, -1)
    )
    above_rows = shifted_2(attended[band_rows - SH :], "lat", 1)
    attended = jnp.concatenate([above_rows, attended[: band_rows - SH]], axis=0)
    west_cols = shifted_2(attended[:, band_cols - SW :], "lon", 1)
    attended = jnp.concatenate([west_cols, attended[:, : band_cols - SW]], axis=1)
    if whole_weights:
        attended, near, far = lax.optimization_barrier((attended, near, far))
        far = first_swap([far])
        near = second_swap(*near)
    stream = stream + project(attended, fine_out)
    hidden = jax.nn.gelu(
        project(layer_norm(stream).astype(jnp.bfloat16), fine_up), approximate=False
    ).astype(jnp.bfloat16)
    if whole_weights:
        hidden, far, middle = lax.optimization_barrier((hidden, far, middle))
        middle = first_swap([middle])
        far = second_swap(*far)
    skip_tokens = (stream + project(hidden, fine_down)).astype(jnp.bfloat16)
    skip_tokens = lax.optimization_barrier(skip_tokens)
    coarse_rows, coarse_cols = (band_rows // 2, band_cols // 2)
    wins = (coarse_rows // WH, WH, 2, coarse_cols // WW, WW, 2)
    merged = (
        skip_tokens.reshape(wins + (-1,))
        .transpose(0, 3, 1, 4, 2, 5, 6)
        .reshape(coarse_rows * coarse_cols, -1)
    )
    merged = lax.optimization_barrier(merged)
    coarse = project(
        layer_norm(merged.astype(jnp.float32)).astype(jnp.bfloat16), merge_weight
    ).astype(jnp.bfloat16)
    coarse_float = coarse.astype(jnp.float32)
    if whole_weights:
        coarse_float, middle = lax.optimization_barrier((coarse_float, middle))
        mlp_moved = (near, far, second_swap(*middle))
        level_state = local_level(
            coarse_float, attend_moved, mlp_moved, coarse_qkv, coarse_out, coarse_up, coarse_down
        )
    else:
        coarse_float = (
            coarse_float.reshape(wins[0], wins[3], WH, WW, -1)
            .transpose(0, 2, 1, 3, 4)
            .reshape(coarse_rows, coarse_cols, -1)
        )
        gathered = lax.all_gather(
            layer_norm(coarse_float).astype(jnp.bfloat16), "lon", axis=1, tiled=True
        )
        level_state = coarse_float + lax.psum_scatter(
            head_terms(gathered, coarse_qkv, coarse_out).astype(jnp.bfloat16),
            "lon",
            scatter_dimension=1,
            tiled=True,
        ).astype(jnp.float32)
        unit_total = unit_terms(
            lax.all_gather(layer_norm(level_state).astype(jnp.bfloat16), "lon", axis=1, tiled=True),
            coarse_up,
            coarse_down,
        )
        level_state = (
            level_state
            + lax.psum_scatter(
                unit_total.astype(jnp.bfloat16), "lon", scatter_dimension=1, tiled=True
            ).astype(jnp.float32)
        ).astype(jnp.bfloat16)
        level_state = (
            level_state.reshape(wins[0], WH, wins[3], WW, -1)
            .transpose(0, 2, 1, 3, 4)
            .reshape(coarse_rows * coarse_cols, -1)
        )
    expanded = project(level_state, split_weight)
    expanded = (
        expanded.reshape(wins[0], wins[3], WH, WW, 2, 2, -1)
        .transpose(0, 2, 4, 1, 3, 5, 6)
        .reshape(band_rows, band_cols, -1)
    )
    return (skip_tokens.astype(jnp.float32) + layer_norm(expanded)).astype(jnp.bfloat16)


def solution(mesh):
    return jax.shard_map(
        per_device,
        mesh=mesh,
        in_specs=(
            P("lat", "lon", None),
            P(),
            P(),
            P(),
            P(),
            P(),
            P(None, "lon"),
            P(None, "lon"),
            P(None, "lon"),
            P(None, "lon"),
            P(),
        ),
        out_specs=P("lat", "lon", None),
        check_vma=False,
    )
```

```python
import functools

import jax
import jax.numpy as jnp
from jax import lax
from jax.experimental import pallas as pl
from jax.experimental.pallas import tpu as pltpu
from jax.sharding import PartitionSpec as P

HD = 64
WH = 6
WW = 12
SH = 3
SW = 6


def shifted_2(block, axis, distance):
    devices = range(lax.axis_size(axis))
    route = [((i - distance) % len(devices), i) for i in devices]
    return lax.ppermute(block, axis, route)


def layer_norm(values):
    average = jnp.mean(values, axis=-1, keepdims=True)
    centred = values - average
    spread = jnp.mean(centred * centred, axis=-1, keepdims=True)
    return centred * lax.rsqrt(spread + 1e-05)


def project(operand, matrix):
    flattened = operand.reshape(-1, operand.shape[-1])
    result = jnp.dot(flattened, matrix, preferred_element_type=jnp.float32)
    return result.reshape(operand.shape[:-1] + (matrix.shape[1],))


def project_back(operand, matrix):
    flattened = operand.reshape(-1, operand.shape[-1])
    result = lax.dot_general(
        flattened, matrix, (((1,), (1,)), ((), ())), preferred_element_type=jnp.float32
    )
    return result.reshape(operand.shape[:-1] + (matrix.shape[0],))


def window_attend(packed, labels, head_count):
    row_count, col_count = (packed.shape[0], packed.shape[1])
    row_wins, col_wins = (row_count // WH, col_count // WW)
    grouped = packed.reshape(row_wins, WH, col_wins, WW, head_count, 3, HD)
    grouped = grouped.transpose(0, 2, 4, 5, 1, 3, 6).reshape(
        row_wins, col_wins, head_count, 3, WH * WW, HD
    )
    queries = grouped[:, :, :, 0]
    key_rows = grouped[:, :, :, 1]
    value_rows = grouped[:, :, :, 2]
    scores = jnp.einsum(
        "abhqd,abhkd->abhqk", queries, key_rows, preferred_element_type=jnp.float32
    ) * HD ** (-0.5)
    if labels is not None:
        token_labels = jnp.broadcast_to(
            labels.reshape(row_wins, WH, 1), (row_wins, WH, WW)
        ).reshape(row_wins, 1, 1, WH * WW)
        same_region = token_labels[..., :, None] == token_labels[..., None, :]
        scores = jnp.where(same_region, scores, -jnp.inf)
    row_max = jnp.max(scores, axis=-1, keepdims=True)
    weights = jnp.exp(scores - row_max)
    normed_probs = (weights / jnp.sum(weights, axis=-1, keepdims=True)).astype(jnp.bfloat16)
    mixture = jnp.einsum(
        "abhqk,abhkd->abhqd", normed_probs, value_rows, preferred_element_type=jnp.float32
    ).astype(jnp.bfloat16)
    mixture = mixture.reshape(row_wins, col_wins, head_count, WH, WW, HD).transpose(
        0, 3, 1, 4, 2, 5
    )
    return mixture.reshape(row_count, col_count, head_count * HD)


def head_terms(normed, qkv_cols, out_cols):
    head_count = qkv_cols.shape[1] // (3 * HD)
    packed = project(normed, qkv_cols).astype(jnp.bfloat16)
    return project_back(window_attend(packed, None, head_count), out_cols)


def unit_terms(normed, up_cols, down_cols):
    hidden = jax.nn.gelu(project(normed, up_cols), approximate=False).astype(jnp.bfloat16)
    return project_back(hidden, down_cols)


BLK = 128
NT = (((1,), (1,)), ((), ()))


def softmax_mix(q, k, v, bias):
    scores = lax.dot_general(q, k, NT, preferred_element_type=jnp.float32) * HD ** (-0.5)
    if bias is not None:
        scores = scores + bias
    weights = jnp.exp(scores - jnp.max(scores, axis=-1, keepdims=True))
    probs = weights / jnp.sum(weights, axis=-1, keepdims=True)
    return jnp.dot(probs.astype(jnp.bfloat16), v, preferred_element_type=jnp.float32)


def fine_kernel(heads, qkv_ref, bias_ref, out_ref):
    bias = bias_ref[0]
    for pair in range(heads // 2):
        block = qkv_ref[0, :, pair * 6 * HD : (pair + 1) * 6 * HD]
        parts = [block[:, i * HD : (i + 1) * HD] for i in range(6)]
        mixed = [softmax_mix(*parts[3 * i : 3 * i + 3], bias) for i in range(2)]
        out_ref[0, :, pair * 2 * HD : (pair + 1) * 2 * HD] = jnp.concatenate(
            mixed, axis=1
        ).astype(jnp.bfloat16)


def fine_attend(qkv, bias):
    wins, size, width = qkv.shape
    per_row = wins // bias.shape[0]
    return pl.pallas_call(
        functools.partial(fine_kernel, width // (3 * HD)),
        out_shape=jax.ShapeDtypeStruct((wins, size, width // 3), jnp.bfloat16),
        grid=(wins,),
        in_specs=[
            pl.BlockSpec((1, size, width), lambda w: (w, 0, 0)),
            pl.BlockSpec((1, size, size), lambda w: (w // per_row, 0, 0)),
        ],
        out_specs=pl.BlockSpec((1, size, width // 3), lambda w: (w, 0, 0)),
        compiler_params=pltpu.CompilerParams(vmem_limit_bytes=32 * 2**20),
        cost_estimate=pl.CostEstimate(
            flops=4 * wins * size * size * width // 3,
            bytes_accessed=wins * size * width * 3,
            transcendentals=wins * size * size * width // (3 * HD),
        ),
    )(qkv, bias)


def fine_mlp_kernel(tokens_ref, attended_ref, out_ref, up_ref, down_ref, skip_ref, stream_ref, normed_ref):
    step = pl.program_id(0)

    @pl.when(step == 0)
    def _():
        stream = tokens_ref[...].astype(jnp.float32) + jnp.dot(
            attended_ref[...], out_ref[...], preferred_element_type=jnp.float32
        )
        stream_ref[...] = stream
        normed_ref[...] = layer_norm(stream).astype(jnp.bfloat16)

    wide = jnp.dot(normed_ref[...], up_ref[...], preferred_element_type=jnp.float32)
    hidden = (0.5 * wide * (1.0 + lax.erf(wide * 0.5**0.5))).astype(jnp.bfloat16)
    stream_ref[...] += jnp.dot(hidden, down_ref[...], preferred_element_type=jnp.float32)

    @pl.when(step == pl.num_programs(0) - 1)
    def _():
        skip_ref[...] = stream_ref[...].astype(jnp.bfloat16)


def fine_mlp(tokens, attended, out, up, down):
    count, width = tokens.shape
    hidden = up.shape[1]
    tile = 512
    whole = pl.BlockSpec((count, width), lambda s: (0, 0))
    return pl.pallas_call(
        fine_mlp_kernel,
        out_shape=jax.ShapeDtypeStruct((count, width), jnp.bfloat16),
        grid=(hidden // tile,),
        in_specs=[
            whole,
            whole,
            pl.BlockSpec((width, width), lambda s: (0, 0)),
            pl.BlockSpec((width, tile), lambda s: (0, s)),
            pl.BlockSpec((tile, width), lambda s: (s, 0)),
        ],
        out_specs=whole,
        scratch_shapes=[
            pltpu.VMEM((count, width), jnp.float32),
            pltpu.VMEM((count, width), jnp.bfloat16),
        ],
        compiler_params=pltpu.CompilerParams(vmem_limit_bytes=32 * 2**20),
        cost_estimate=pl.CostEstimate(
            flops=2 * count * width * (width + 2 * hidden),
            bytes_accessed=2 * width * (width + 2 * hidden),
            transcendentals=count * hidden,
        ),
    )(tokens, attended, out, up, down)


def coarse_attend_kernel(x_ref, qkv_ref, rows_ref, a0_ref, a1_ref, b0_ref, b1_ref, own_ref, peer_ref, sum_ref):
    lat = lax.axis_index("lat")
    count, width = x_ref.shape
    size, deep = WH * WW, width // 4
    shifts = a0_ref.shape[0] // 2
    halves_a, halves_b = (a0_ref, a1_ref), (b0_ref, b1_ref)

    def mixed_heads(qkv):
        rows = []
        for w in range(count // size):
            block = qkv[w * size : (w + 1) * size].astype(jnp.bfloat16)
            parts = [block[:, i * HD : (i + 1) * HD] for i in range(6)]
            rows.append(
                jnp.concatenate(
                    [softmax_mix(*parts[3 * i : 3 * i + 3], None) for i in range(2)], axis=1
                )
            )
        return jnp.concatenate(rows, axis=0).astype(jnp.bfloat16)

    def columns(j):
        return pl.ds(pl.multiple_of((lat ^ j) * deep, deep), deep)

    mixed = mixed_heads(jnp.dot(x_ref[...], qkv_ref[...], preferred_element_type=jnp.float32))
    sum_ref[...] = lax.dot_general(mixed, rows_ref[...], NT, preferred_element_type=jnp.float32)
    for s in range(shifts):
        qkv = None
        for j in range(4):
            first = halves_a[j // 2][(j % 2) * shifts + s]
            second = halves_b[j % 2][(j // 2) * shifts + s]
            block = jnp.concatenate([first[:deep], first[deep:], second[:deep]], axis=1)
            term = jnp.dot(x_ref[:, columns(j)], block, preferred_element_type=jnp.float32)
            qkv = term if qkv is None else qkv + term
        mixed = mixed_heads(qkv)
        for j in range(4):
            out_rows = halves_b[j % 2][(j // 2) * shifts + s][deep:]
            sum_ref[:, columns(j)] += lax.dot_general(
                mixed, out_rows, NT, preferred_element_type=jnp.float32
            )
    own_ref[...] = sum_ref[: count // 2]
    peer_ref[...] = sum_ref[count // 2 :].astype(jnp.bfloat16)


def coarse_attend(x, qkv, out, moved):
    count, width = x.shape
    whole = pl.BlockSpec(memory_space=pltpu.VMEM)
    return pl.pallas_call(
        coarse_attend_kernel,
        out_shape=(
            jax.ShapeDtypeStruct((count // 2, width), jnp.float32),
            jax.ShapeDtypeStruct((count // 2, width), jnp.bfloat16),
        ),
        in_specs=[whole] * 7,
        out_specs=(whole, whole),
        scratch_shapes=[pltpu.VMEM((count, width), jnp.float32)],
        compiler_params=pltpu.CompilerParams(vmem_limit_bytes=40 * 2**20),
        cost_estimate=pl.CostEstimate(
            flops=4 * count * width * width,
            bytes_accessed=4 * width * width,
            transcendentals=count * WH * WW * 8,
        ),
    )(x, qkv, out, *moved)


def coarse_mlp_kernel(x_ref, base_ref, *refs):
    ups, downs, out_ref = refs[: len(refs) // 2], refs[len(refs) // 2 : -1], refs[-1]

    @pl.when(pl.program_id(0) == 0)
    def _():
        out_ref[...] = base_ref[...]

    def joined(parts):
        parts = [part[...].reshape(part.shape[-2:]) for part in parts]
        return parts[0] if len(parts) == 1 else jnp.concatenate(parts, axis=1)

    wide = jnp.dot(x_ref[...], joined(ups), preferred_element_type=jnp.float32)
    hidden = (0.5 * wide * (1.0 + lax.erf(wide * 0.5**0.5))).astype(jnp.bfloat16)
    out_ref[...] += lax.dot_general(hidden, joined(downs), NT, preferred_element_type=jnp.float32)


def coarse_mlp(x, base, steps, operands, specs):
    count, width = x.shape
    whole = pl.BlockSpec((count, width), lambda s: (0, 0))
    hidden = steps * 4 * BLK
    return pl.pallas_call(
        coarse_mlp_kernel,
        out_shape=jax.ShapeDtypeStruct((count, width), jnp.float32),
        grid=(steps,),
        in_specs=[whole, whole] + specs,
        out_specs=whole,
        compiler_params=pltpu.CompilerParams(vmem_limit_bytes=40 * 2**20),
        cost_estimate=pl.CostEstimate(
            flops=4 * count * width * hidden,
            bytes_accessed=4 * width * hidden,
            transcendentals=count * hidden,
        ),
    )(x, base, *operands)


def own_mlp(x, up, down):
    base = jnp.zeros(x.shape, jnp.float32)
    return coarse_mlp(x, base, 1, [up, down], [pl.BlockSpec(up.shape, lambda s: (0, 0))] * 2)


def moved_mlp(x, base, moved):
    a0, a1, b0, b1 = moved
    shifts = a0.shape[0] // 2
    low = pl.BlockSpec((1,) + a0.shape[1:], lambda s: (s, 0, 0))
    high = pl.BlockSpec((1,) + a0.shape[1:], lambda s: (shifts + s, 0, 0))
    operands = [a0, a0, a1, a1, b0, b1, b0, b1]
    return coarse_mlp(x, base, shifts, operands, [low, high, low, high, low, low, high, high])


def swapped(block, axis, bit):
    return lax.ppermute(block, axis, [(i, i ^ bit) for i in range(lax.axis_size(axis))])


def along_lon(a, b, shifts):
    lons = lax.axis_size("lon")
    both = jnp.stack([a, b])
    return [
        lax.ppermute(both, "lon", [(i, (i + shift) % lons) for i in range(lons)])
        for shift in shifts
    ]


def first_swap(got):
    a = jnp.stack([one[0] for one in got])
    b = jnp.stack([one[1] for one in got])
    return (a, swapped(a, "lat", 1), b, swapped(b, "lat", 2))


def second_swap(a, ax, b, by):
    a0, b0 = jnp.concatenate([a, ax], axis=0), jnp.concatenate([b, by], axis=0)
    return (a0, swapped(a0, "lat", 2), b0, swapped(b0, "lat", 1))


def level_parts(qkv, out, up, down):
    lat = lax.axis_index("lat")
    deep = qkv.shape[0] // 4
    qkv = lax.dynamic_slice_in_dim(qkv, lat * deep, deep, 0)
    out = lax.dynamic_slice_in_dim(out, lat * deep, deep, 0)
    first = jnp.concatenate([qkv[:, :BLK], qkv[:, BLK : 2 * BLK]], axis=0)
    second = jnp.concatenate([qkv[:, 2 * BLK :], out], axis=0)
    up = lax.dynamic_slice_in_dim(up, lat * BLK, BLK, 1)
    return (first, second), (up, lax.dynamic_slice_in_dim(down, lat * BLK, BLK, 1))


def local_level(tokens, attend_moved, near, middle, far, qkv, out, up, down):
    count = tokens.shape[0]

    def shared(values):
        normed = layer_norm(values).astype(jnp.bfloat16)
        return jnp.concatenate([normed, swapped(normed, "lon", 1)], axis=0)

    own, peer = coarse_attend(shared(tokens), qkv, out, attend_moved)
    peer, far, middle = lax.optimization_barrier((peer, far, middle))
    middle = first_swap([middle])
    far = second_swap(*far)
    tokens = tokens + own + swapped(peer, "lon", 1).astype(jnp.float32)
    both = shared(tokens)
    both, middle = lax.optimization_barrier((both, middle))
    middle = second_swap(*middle)
    total = own_mlp(both, up, down)
    for moved in (near, far, middle):
        total = moved_mlp(both, total, moved)
    peer = swapped(total[count:].astype(jnp.bfloat16), "lon", 1)
    return (tokens + total[:count] + peer.astype(jnp.float32)).astype(jnp.bfloat16)


def per_device(
    tokens,
    fine_qkv,
    fine_out,
    fine_up,
    fine_down,
    merge_weight,
    coarse_qkv,
    coarse_out,
    coarse_up,
    coarse_down,
    split_weight,
):
    band_rows, band_cols = (tokens.shape[0], tokens.shape[1])
    total_rows = band_rows * lax.axis_size("lat")
    lat_index = lax.axis_index("lat")
    whole_weights = (
        lax.axis_size("lat") == 4 and coarse_up.shape[1] == 4 * BLK and coarse_qkv.shape[1] == 3 * BLK
    )
    if whole_weights:
        attend_part, mlp_part = level_parts(coarse_qkv, coarse_out, coarse_up, coarse_down)
    below_rows = shifted_2(tokens[:SH], "lat", -1)
    shifted = jnp.concatenate([tokens[SH:], below_rows], axis=0)
    east_cols = shifted_2(shifted[:, :SW], "lon", -1)
    if whole_weights:
        east_cols, attend_part, mlp_part = lax.optimization_barrier((east_cols, attend_part, mlp_part))
        attend_moved = along_lon(*attend_part, (2, 4, 6))
    shifted = jnp.concatenate([shifted[:, SW:], east_cols], axis=1)
    anchor = (lat_index * band_rows + jnp.arange(band_rows, dtype=jnp.int32) + SH) % total_rows
    labels = (anchor < SH).astype(jnp.int32)
    row_wins, col_wins = (band_rows // WH, band_cols // WW)
    window_labels = jnp.repeat(labels.reshape(row_wins, WH), WW, axis=1)
    same_region = window_labels[:, :, None] == window_labels[:, None, :]
    bias = jnp.where(same_region, 0.0, -jnp.inf).astype(jnp.float32)
    shifted = (
        shifted.reshape(row_wins, WH, col_wins, WW, -1)
        .transpose(0, 2, 1, 3, 4)
        .reshape(row_wins * col_wins, WH * WW, -1)
    )
    shifted = lax.optimization_barrier(shifted)
    normed = layer_norm(shifted.astype(jnp.float32)).astype(jnp.bfloat16)
    packed = project(normed, fine_qkv).astype(jnp.bfloat16)
    if whole_weights:
        packed, mlp_part = lax.optimization_barrier((packed, mlp_part))
        (near,) = along_lon(*mlp_part, (2,))
    attended = fine_attend(packed, bias)
    if whole_weights:
        attended, attend_moved = lax.optimization_barrier((attended, attend_moved))
        attend_moved = first_swap(attend_moved)
    attended = (
        attended.reshape(row_wins, col_wins, WH, WW, -1)
        .transpose(0, 2, 1, 3, 4)
        .reshape(band_rows, band_cols, -1)
    )
    above_rows = shifted_2(attended[band_rows - SH :], "lat", 1)
    attended = jnp.concatenate([above_rows, attended[: band_rows - SH]], axis=0)
    west_cols = shifted_2(attended[:, band_cols - SW :], "lon", 1)
    attended = jnp.concatenate([west_cols, attended[:, : band_cols - SW]], axis=1)
    if whole_weights:
        attended, attend_moved, mlp_part = lax.optimization_barrier((attended, attend_moved, mlp_part))
        far, middle = along_lon(*mlp_part, (6, 4))
        attend_moved = second_swap(*attend_moved)
    skip_tokens = fine_mlp(
        tokens.reshape(band_rows * band_cols, -1),
        attended.reshape(band_rows * band_cols, -1),
        fine_out,
        fine_up,
        fine_down,
    )
    if whole_weights:
        skip_tokens, near = lax.optimization_barrier((skip_tokens, near))
        near = first_swap([near])
    skip_tokens = lax.optimization_barrier(skip_tokens).reshape(tokens.shape)
    coarse_rows, coarse_cols = (band_rows // 2, band_cols // 2)
    wins = (coarse_rows // WH, WH, 2, coarse_cols // WW, WW, 2)
    merged = (
        skip_tokens.reshape(wins + (-1,))
        .transpose(0, 3, 1, 4, 2, 5, 6)
        .reshape(coarse_rows * coarse_cols, -1)
    )
    merged = lax.optimization_barrier(merged)
    coarse = project(
        layer_norm(merged.astype(jnp.float32)).astype(jnp.bfloat16), merge_weight
    ).astype(jnp.bfloat16)
    coarse_float = coarse.astype(jnp.float32)
    if whole_weights:
        coarse_float, near, far = lax.optimization_barrier((coarse_float, near, far))
        far = first_swap([far])
        near = second_swap(*near)
        level_state = local_level(
            coarse_float, attend_moved, near, middle, far, coarse_qkv, coarse_out, coarse_up, coarse_down
        )
    else:
        coarse_float = (
            coarse_float.reshape(wins[0], wins[3], WH, WW, -1)
            .transpose(0, 2, 1, 3, 4)
            .reshape(coarse_rows, coarse_cols, -1)
        )
        gathered = lax.all_gather(
            layer_norm(coarse_float).astype(jnp.bfloat16), "lon", axis=1, tiled=True
        )
        level_state = coarse_float + lax.psum_scatter(
            head_terms(gathered, coarse_qkv, coarse_out).astype(jnp.bfloat16),
            "lon",
            scatter_dimension=1,
            tiled=True,
        ).astype(jnp.float32)
        unit_total = unit_terms(
            lax.all_gather(layer_norm(level_state).astype(jnp.bfloat16), "lon", axis=1, tiled=True),
            coarse_up,
            coarse_down,
        )
        level_state = (
            level_state
            + lax.psum_scatter(
                unit_total.astype(jnp.bfloat16), "lon", scatter_dimension=1, tiled=True
            ).astype(jnp.float32)
        ).astype(jnp.bfloat16)
        level_state = (
            level_state.reshape(wins[0], WH, wins[3], WW, -1)
            .transpose(0, 2, 1, 3, 4)
            .reshape(coarse_rows * coarse_cols, -1)
        )
    expanded = project(level_state, split_weight)
    expanded = (
        expanded.reshape(wins[0], wins[3], WH, WW, 2, 2, -1)
        .transpose(0, 2, 4, 1, 3, 5, 6)
        .reshape(band_rows, band_cols, -1)
    )
    return (skip_tokens.astype(jnp.float32) + layer_norm(expanded)).astype(jnp.bfloat16)


def solution(mesh):
    return jax.shard_map(
        per_device,
        mesh=mesh,
        in_specs=(
            P("lat", "lon", None),
            P(),
            P(),
            P(),
            P(),
            P(),
            P(None, "lon"),
            P(None, "lon"),
            P(None, "lon"),
            P(None, "lon"),
            P(),
        ),
        out_specs=P("lat", "lon", None),
        check_vma=False,
    )
```

```python
import functools

import jax
import jax.numpy as jnp
from jax import lax
from jax.experimental import pallas as pl
from jax.experimental.pallas import tpu as pltpu
from jax.sharding import PartitionSpec as P

HD = 64
WH = 6
WW = 12
SH = 3
SW = 6


def shifted_2(block, axis, distance):
    devices = range(lax.axis_size(axis))
    route = [((i - distance) % len(devices), i) for i in devices]
    return lax.ppermute(block, axis, route)


def layer_norm(values):
    average = jnp.mean(values, axis=-1, keepdims=True)
    centred = values - average
    spread = jnp.mean(centred * centred, axis=-1, keepdims=True)
    return centred * lax.rsqrt(spread + 1e-05)


def project(operand, matrix):
    flattened = operand.reshape(-1, operand.shape[-1])
    result = jnp.dot(flattened, matrix, preferred_element_type=jnp.float32)
    return result.reshape(operand.shape[:-1] + (matrix.shape[1],))


def project_back(operand, matrix):
    flattened = operand.reshape(-1, operand.shape[-1])
    result = lax.dot_general(
        flattened, matrix, (((1,), (1,)), ((), ())), preferred_element_type=jnp.float32
    )
    return result.reshape(operand.shape[:-1] + (matrix.shape[0],))


def window_attend(packed, labels, head_count):
    row_count, col_count = (packed.shape[0], packed.shape[1])
    row_wins, col_wins = (row_count // WH, col_count // WW)
    grouped = packed.reshape(row_wins, WH, col_wins, WW, head_count, 3, HD)
    grouped = grouped.transpose(0, 2, 4, 5, 1, 3, 6).reshape(
        row_wins, col_wins, head_count, 3, WH * WW, HD
    )
    queries = grouped[:, :, :, 0]
    key_rows = grouped[:, :, :, 1]
    value_rows = grouped[:, :, :, 2]
    scores = jnp.einsum(
        "abhqd,abhkd->abhqk", queries, key_rows, preferred_element_type=jnp.float32
    ) * HD ** (-0.5)
    if labels is not None:
        token_labels = jnp.broadcast_to(
            labels.reshape(row_wins, WH, 1), (row_wins, WH, WW)
        ).reshape(row_wins, 1, 1, WH * WW)
        same_region = token_labels[..., :, None] == token_labels[..., None, :]
        scores = jnp.where(same_region, scores, -jnp.inf)
    row_max = jnp.max(scores, axis=-1, keepdims=True)
    weights = jnp.exp(scores - row_max)
    normed_probs = (weights / jnp.sum(weights, axis=-1, keepdims=True)).astype(jnp.bfloat16)
    mixture = jnp.einsum(
        "abhqk,abhkd->abhqd", normed_probs, value_rows, preferred_element_type=jnp.float32
    ).astype(jnp.bfloat16)
    mixture = mixture.reshape(row_wins, col_wins, head_count, WH, WW, HD).transpose(
        0, 3, 1, 4, 2, 5
    )
    return mixture.reshape(row_count, col_count, head_count * HD)


def head_terms(normed, qkv_cols, out_cols):
    head_count = qkv_cols.shape[1] // (3 * HD)
    packed = project(normed, qkv_cols).astype(jnp.bfloat16)
    return project_back(window_attend(packed, None, head_count), out_cols)


def unit_terms(normed, up_cols, down_cols):
    hidden = jax.nn.gelu(project(normed, up_cols), approximate=False).astype(jnp.bfloat16)
    return project_back(hidden, down_cols)


BLK = 128
NT = (((1,), (1,)), ((), ()))


def softmax_mix(q, k, v, bias):
    scores = lax.dot_general(q, k, NT, preferred_element_type=jnp.float32) * HD ** (-0.5)
    if bias is not None:
        scores = scores + bias
    weights = jnp.exp(scores - jnp.max(scores, axis=-1, keepdims=True))
    probs = weights / jnp.sum(weights, axis=-1, keepdims=True)
    return jnp.dot(probs.astype(jnp.bfloat16), v, preferred_element_type=jnp.float32)


def fine_kernel(heads, qkv_ref, bias_ref, out_ref):
    bias = bias_ref[0]
    for pair in range(heads // 2):
        block = qkv_ref[0, :, pair * 6 * HD : (pair + 1) * 6 * HD]
        parts = [block[:, i * HD : (i + 1) * HD] for i in range(6)]
        mixed = [softmax_mix(*parts[3 * i : 3 * i + 3], bias) for i in range(2)]
        out_ref[0, :, pair * 2 * HD : (pair + 1) * 2 * HD] = jnp.concatenate(
            mixed, axis=1
        ).astype(jnp.bfloat16)


def fine_attend(qkv, bias):
    wins, size, width = qkv.shape
    per_row = wins // bias.shape[0]
    return pl.pallas_call(
        functools.partial(fine_kernel, width // (3 * HD)),
        out_shape=jax.ShapeDtypeStruct((wins, size, width // 3), jnp.bfloat16),
        grid=(wins,),
        in_specs=[
            pl.BlockSpec((1, size, width), lambda w: (w, 0, 0)),
            pl.BlockSpec((1, size, size), lambda w: (w // per_row, 0, 0)),
        ],
        out_specs=pl.BlockSpec((1, size, width // 3), lambda w: (w, 0, 0)),
        compiler_params=pltpu.CompilerParams(vmem_limit_bytes=32 * 2**20),
        cost_estimate=pl.CostEstimate(
            flops=4 * wins * size * size * width // 3,
            bytes_accessed=wins * size * width * 3,
            transcendentals=wins * size * size * width // (3 * HD),
        ),
    )(qkv, bias)


def fine_mlp_kernel(tokens_ref, attended_ref, out_ref, up_ref, down_ref, skip_ref, stream_ref, normed_ref):
    step = pl.program_id(0)

    @pl.when(step == 0)
    def _():
        stream = tokens_ref[...].astype(jnp.float32) + jnp.dot(
            attended_ref[...], out_ref[...], preferred_element_type=jnp.float32
        )
        stream_ref[...] = stream
        normed_ref[...] = layer_norm(stream).astype(jnp.bfloat16)

    wide = jnp.dot(normed_ref[...], up_ref[...], preferred_element_type=jnp.float32)
    hidden = (0.5 * wide * (1.0 + lax.erf(wide * 0.5**0.5))).astype(jnp.bfloat16)
    stream_ref[...] += jnp.dot(hidden, down_ref[...], preferred_element_type=jnp.float32)

    @pl.when(step == pl.num_programs(0) - 1)
    def _():
        skip_ref[...] = stream_ref[...].astype(jnp.bfloat16)


def fine_mlp(tokens, attended, out, up, down):
    count, width = tokens.shape
    hidden = up.shape[1]
    tile = 512
    whole = pl.BlockSpec((count, width), lambda s: (0, 0))
    return pl.pallas_call(
        fine_mlp_kernel,
        out_shape=jax.ShapeDtypeStruct((count, width), jnp.bfloat16),
        grid=(hidden // tile,),
        in_specs=[
            whole,
            whole,
            pl.BlockSpec((width, width), lambda s: (0, 0)),
            pl.BlockSpec((width, tile), lambda s: (0, s)),
            pl.BlockSpec((tile, width), lambda s: (s, 0)),
        ],
        out_specs=whole,
        scratch_shapes=[
            pltpu.VMEM((count, width), jnp.float32),
            pltpu.VMEM((count, width), jnp.bfloat16),
        ],
        compiler_params=pltpu.CompilerParams(vmem_limit_bytes=32 * 2**20),
        cost_estimate=pl.CostEstimate(
            flops=2 * count * width * (width + 2 * hidden),
            bytes_accessed=2 * width * (width + 2 * hidden),
            transcendentals=count * hidden,
        ),
    )(tokens, attended, out, up, down)


def split_join_kernel(level_ref, weight_ref, skip_ref, out_ref):
    width = out_ref.shape[1] // 4
    for i in range(4):
        columns = slice(i * width, (i + 1) * width)
        expanded = jnp.dot(
            level_ref[...], weight_ref[:, columns], preferred_element_type=jnp.float32
        )
        joined = skip_ref[:, columns].astype(jnp.float32) + layer_norm(expanded)
        out_ref[:, columns] = joined.astype(jnp.bfloat16)


def split_join(level, weight, merged):
    whole = pl.BlockSpec(memory_space=pltpu.VMEM)
    return pl.pallas_call(
        split_join_kernel,
        out_shape=jax.ShapeDtypeStruct(merged.shape, jnp.bfloat16),
        in_specs=[whole] * 3,
        out_specs=whole,
        compiler_params=pltpu.CompilerParams(vmem_limit_bytes=32 * 2**20),
        cost_estimate=pl.CostEstimate(
            flops=2 * merged.shape[0] * weight.shape[0] * weight.shape[1],
            bytes_accessed=2 * weight.shape[0] * weight.shape[1],
            transcendentals=0,
        ),
    )(level, weight, merged)


def coarse_attend_kernel(x_ref, qkv_ref, rows_ref, a0_ref, a1_ref, b0_ref, b1_ref, own_ref, peer_ref, sum_ref):
    lat = lax.axis_index("lat")
    count, width = x_ref.shape
    size, deep = WH * WW, width // 4
    shifts = a0_ref.shape[0] // 2
    halves_a, halves_b = (a0_ref, a1_ref), (b0_ref, b1_ref)

    def mixed_heads(qkv):
        rows = []
        for w in range(count // size):
            block = qkv[w * size : (w + 1) * size].astype(jnp.bfloat16)
            parts = [block[:, i * HD : (i + 1) * HD] for i in range(6)]
            rows.append(
                jnp.concatenate(
                    [softmax_mix(*parts[3 * i : 3 * i + 3], None) for i in range(2)], axis=1
                )
            )
        return jnp.concatenate(rows, axis=0).astype(jnp.bfloat16)

    def columns(j):
        return pl.ds(pl.multiple_of((lat ^ j) * deep, deep), deep)

    mixed = mixed_heads(jnp.dot(x_ref[...], qkv_ref[...], preferred_element_type=jnp.float32))
    sum_ref[...] = lax.dot_general(mixed, rows_ref[...], NT, preferred_element_type=jnp.float32)
    for s in range(shifts):
        qkv = None
        for j in range(4):
            first = halves_a[j // 2][(j % 2) * shifts + s]
            second = halves_b[j % 2][(j // 2) * shifts + s]
            block = jnp.concatenate([first[:deep], first[deep:], second[:deep]], axis=1)
            term = jnp.dot(x_ref[:, columns(j)], block, preferred_element_type=jnp.float32)
            qkv = term if qkv is None else qkv + term
        mixed = mixed_heads(qkv)
        for j in range(4):
            out_rows = halves_b[j % 2][(j // 2) * shifts + s][deep:]
            sum_ref[:, columns(j)] += lax.dot_general(
                mixed, out_rows, NT, preferred_element_type=jnp.float32
            )
    own_ref[...] = sum_ref[: count // 2]
    peer_ref[...] = sum_ref[count // 2 :].astype(jnp.bfloat16)


def coarse_attend(x, qkv, out, moved):
    count, width = x.shape
    whole = pl.BlockSpec(memory_space=pltpu.VMEM)
    return pl.pallas_call(
        coarse_attend_kernel,
        out_shape=(
            jax.ShapeDtypeStruct((count // 2, width), jnp.float32),
            jax.ShapeDtypeStruct((count // 2, width), jnp.bfloat16),
        ),
        in_specs=[whole] * 7,
        out_specs=(whole, whole),
        scratch_shapes=[pltpu.VMEM((count, width), jnp.float32)],
        compiler_params=pltpu.CompilerParams(vmem_limit_bytes=40 * 2**20),
        cost_estimate=pl.CostEstimate(
            flops=4 * count * width * width,
            bytes_accessed=4 * width * width,
            transcendentals=count * WH * WW * 8,
        ),
    )(x, qkv, out, *moved)


def coarse_mlp_kernel(x_ref, base_ref, *refs):
    ups, downs, out_ref = refs[: len(refs) // 2], refs[len(refs) // 2 : -1], refs[-1]

    @pl.when(pl.program_id(0) == 0)
    def _():
        out_ref[...] = base_ref[...]

    def joined(parts):
        parts = [part[...].reshape(part.shape[-2:]) for part in parts]
        return parts[0] if len(parts) == 1 else jnp.concatenate(parts, axis=1)

    wide = jnp.dot(x_ref[...], joined(ups), preferred_element_type=jnp.float32)
    hidden = (0.5 * wide * (1.0 + lax.erf(wide * 0.5**0.5))).astype(jnp.bfloat16)
    out_ref[...] += lax.dot_general(hidden, joined(downs), NT, preferred_element_type=jnp.float32)


def coarse_mlp(x, base, steps, operands, specs):
    count, width = x.shape
    whole = pl.BlockSpec((count, width), lambda s: (0, 0))
    hidden = steps * 4 * BLK
    return pl.pallas_call(
        coarse_mlp_kernel,
        out_shape=jax.ShapeDtypeStruct((count, width), jnp.float32),
        grid=(steps,),
        in_specs=[whole, whole] + specs,
        out_specs=whole,
        compiler_params=pltpu.CompilerParams(vmem_limit_bytes=40 * 2**20),
        cost_estimate=pl.CostEstimate(
            flops=4 * count * width * hidden,
            bytes_accessed=4 * width * hidden,
            transcendentals=count * hidden,
        ),
    )(x, base, *operands)


def own_mlp(x, up, down):
    base = jnp.zeros(x.shape, jnp.float32)
    return coarse_mlp(x, base, 1, [up, down], [pl.BlockSpec(up.shape, lambda s: (0, 0))] * 2)


def moved_mlp(x, base, moved):
    a0, a1, b0, b1 = moved
    shifts = a0.shape[0] // 2
    low = pl.BlockSpec((1,) + a0.shape[1:], lambda s: (s, 0, 0))
    high = pl.BlockSpec((1,) + a0.shape[1:], lambda s: (shifts + s, 0, 0))
    operands = [a0, a0, a1, a1, b0, b1, b0, b1]
    return coarse_mlp(x, base, shifts, operands, [low, high, low, high, low, low, high, high])


def swapped(block, axis, bit):
    return lax.ppermute(block, axis, [(i, i ^ bit) for i in range(lax.axis_size(axis))])


def along_lon(a, b, shifts):
    lons = lax.axis_size("lon")
    both = jnp.stack([a, b])
    return [
        lax.ppermute(both, "lon", [(i, (i + shift) % lons) for i in range(lons)])
        for shift in shifts
    ]


def first_swap(got):
    a = jnp.stack([one[0] for one in got])
    b = jnp.stack([one[1] for one in got])
    return (a, swapped(a, "lat", 1), b, swapped(b, "lat", 2))


def second_swap(a, ax, b, by):
    a0, b0 = jnp.concatenate([a, ax], axis=0), jnp.concatenate([b, by], axis=0)
    return (a0, swapped(a0, "lat", 2), b0, swapped(b0, "lat", 1))


def level_parts(qkv, out, up, down):
    lat = lax.axis_index("lat")
    deep = qkv.shape[0] // 4
    qkv = lax.dynamic_slice_in_dim(qkv, lat * deep, deep, 0)
    out = lax.dynamic_slice_in_dim(out, lat * deep, deep, 0)
    first = jnp.concatenate([qkv[:, :BLK], qkv[:, BLK : 2 * BLK]], axis=0)
    second = jnp.concatenate([qkv[:, 2 * BLK :], out], axis=0)
    up = lax.dynamic_slice_in_dim(up, lat * BLK, BLK, 1)
    return (first, second), (up, lax.dynamic_slice_in_dim(down, lat * BLK, BLK, 1))


def local_level(tokens, attend_moved, near, middle, far, qkv, out, up, down):
    count = tokens.shape[0]

    def shared(values):
        normed = layer_norm(values).astype(jnp.bfloat16)
        return jnp.concatenate([normed, swapped(normed, "lon", 1)], axis=0)

    own, peer = coarse_attend(shared(tokens), qkv, out, attend_moved)
    peer, far, middle = lax.optimization_barrier((peer, far, middle))
    middle = first_swap([middle])
    far = second_swap(*far)
    tokens = tokens + own + swapped(peer, "lon", 1).astype(jnp.float32)
    both = shared(tokens)
    both, middle = lax.optimization_barrier((both, middle))
    middle = second_swap(*middle)
    total = own_mlp(both, up, down)
    for moved in (near, far, middle):
        total = moved_mlp(both, total, moved)
    peer = swapped(total[count:].astype(jnp.bfloat16), "lon", 1)
    return (tokens + total[:count] + peer.astype(jnp.float32)).astype(jnp.bfloat16)


def per_device(
    tokens,
    fine_qkv,
    fine_out,
    fine_up,
    fine_down,
    merge_weight,
    coarse_qkv,
    coarse_out,
    coarse_up,
    coarse_down,
    split_weight,
):
    band_rows, band_cols = (tokens.shape[0], tokens.shape[1])
    total_rows = band_rows * lax.axis_size("lat")
    lat_index = lax.axis_index("lat")
    whole_weights = (
        lax.axis_size("lat") == 4 and coarse_up.shape[1] == 4 * BLK and coarse_qkv.shape[1] == 3 * BLK
    )
    if whole_weights:
        attend_part, mlp_part = level_parts(coarse_qkv, coarse_out, coarse_up, coarse_down)
    below_rows = shifted_2(tokens[:SH], "lat", -1)
    shifted = jnp.concatenate([tokens[SH:], below_rows], axis=0)
    east_cols = shifted_2(shifted[:, :SW], "lon", -1)
    if whole_weights:
        east_cols, attend_part, mlp_part = lax.optimization_barrier((east_cols, attend_part, mlp_part))
        attend_moved = along_lon(*attend_part, (2, 4, 6))
    shifted = jnp.concatenate([shifted[:, SW:], east_cols], axis=1)
    anchor = (lat_index * band_rows + jnp.arange(band_rows, dtype=jnp.int32) + SH) % total_rows
    labels = (anchor < SH).astype(jnp.int32)
    row_wins, col_wins = (band_rows // WH, band_cols // WW)
    window_labels = jnp.repeat(labels.reshape(row_wins, WH), WW, axis=1)
    same_region = window_labels[:, :, None] == window_labels[:, None, :]
    bias = jnp.where(same_region, 0.0, -jnp.inf).astype(jnp.float32)
    shifted = (
        shifted.reshape(row_wins, WH, col_wins, WW, -1)
        .transpose(0, 2, 1, 3, 4)
        .reshape(row_wins * col_wins, WH * WW, -1)
    )
    shifted = lax.optimization_barrier(shifted)
    normed = layer_norm(shifted.astype(jnp.float32)).astype(jnp.bfloat16)
    packed = project(normed, fine_qkv).astype(jnp.bfloat16)
    if whole_weights:
        packed, mlp_part = lax.optimization_barrier((packed, mlp_part))
        (near,) = along_lon(*mlp_part, (2,))
    attended = fine_attend(packed, bias)
    if whole_weights:
        attended, attend_moved = lax.optimization_barrier((attended, attend_moved))
        attend_moved = first_swap(attend_moved)
    attended = (
        attended.reshape(row_wins, col_wins, WH, WW, -1)
        .transpose(0, 2, 1, 3, 4)
        .reshape(band_rows, band_cols, -1)
    )
    above_rows = shifted_2(attended[band_rows - SH :], "lat", 1)
    attended = jnp.concatenate([above_rows, attended[: band_rows - SH]], axis=0)
    west_cols = shifted_2(attended[:, band_cols - SW :], "lon", 1)
    attended = jnp.concatenate([west_cols, attended[:, : band_cols - SW]], axis=1)
    if whole_weights:
        attended, attend_moved, mlp_part = lax.optimization_barrier((attended, attend_moved, mlp_part))
        far, middle = along_lon(*mlp_part, (6, 4))
        attend_moved = second_swap(*attend_moved)
    skip_tokens = fine_mlp(
        tokens.reshape(band_rows * band_cols, -1),
        attended.reshape(band_rows * band_cols, -1),
        fine_out,
        fine_up,
        fine_down,
    )
    if whole_weights:
        skip_tokens, near = lax.optimization_barrier((skip_tokens, near))
        near = first_swap([near])
    skip_tokens = lax.optimization_barrier(skip_tokens).reshape(tokens.shape)
    coarse_rows, coarse_cols = (band_rows // 2, band_cols // 2)
    wins = (coarse_rows // WH, WH, 2, coarse_cols // WW, WW, 2)
    merged = (
        skip_tokens.reshape(wins + (-1,))
        .transpose(0, 3, 1, 4, 2, 5, 6)
        .reshape(coarse_rows * coarse_cols, -1)
    )
    merged = lax.optimization_barrier(merged)
    coarse = project(
        layer_norm(merged.astype(jnp.float32)).astype(jnp.bfloat16), merge_weight
    ).astype(jnp.bfloat16)
    coarse_float = coarse.astype(jnp.float32)
    if whole_weights:
        coarse_float, near, far = lax.optimization_barrier((coarse_float, near, far))
        far = first_swap([far])
        near = second_swap(*near)
        level_state = local_level(
            coarse_float, attend_moved, near, middle, far, coarse_qkv, coarse_out, coarse_up, coarse_down
        )
    else:
        coarse_float = (
            coarse_float.reshape(wins[0], wins[3], WH, WW, -1)
            .transpose(0, 2, 1, 3, 4)
            .reshape(coarse_rows, coarse_cols, -1)
        )
        gathered = lax.all_gather(
            layer_norm(coarse_float).astype(jnp.bfloat16), "lon", axis=1, tiled=True
        )
        level_state = coarse_float + lax.psum_scatter(
            head_terms(gathered, coarse_qkv, coarse_out).astype(jnp.bfloat16),
            "lon",
            scatter_dimension=1,
            tiled=True,
        ).astype(jnp.float32)
        unit_total = unit_terms(
            lax.all_gather(layer_norm(level_state).astype(jnp.bfloat16), "lon", axis=1, tiled=True),
            coarse_up,
            coarse_down,
        )
        level_state = (
            level_state
            + lax.psum_scatter(
                unit_total.astype(jnp.bfloat16), "lon", scatter_dimension=1, tiled=True
            ).astype(jnp.float32)
        ).astype(jnp.bfloat16)
        level_state = (
            level_state.reshape(wins[0], WH, wins[3], WW, -1)
            .transpose(0, 2, 1, 3, 4)
            .reshape(coarse_rows * coarse_cols, -1)
        )
    joined = split_join(level_state, split_weight, merged)
    return (
        joined.reshape(wins[0], wins[3], WH, WW, 2, 2, -1)
        .transpose(0, 2, 4, 1, 3, 5, 6)
        .reshape(tokens.shape)
    )


def solution(mesh):
    return jax.shard_map(
        per_device,
        mesh=mesh,
        in_specs=(
            P("lat", "lon", None),
            P(),
            P(),
            P(),
            P(),
            P(),
            P(None, "lon"),
            P(None, "lon"),
            P(None, "lon"),
            P(None, "lon"),
            P(),
        ),
        out_specs=P("lat", "lon", None),
        check_vma=False,
    )
```
